256 devices in a mesh: group: 8 (over y, x_hi), blk: 32 (over z, x_lo, core).
Axes of the slice: x: 4 (x_hi: 2, x_lo: 2; x = x_hi * 2 + x_lo), y: 4, z: 8, core: 2. Of those that a mesh axis runs over, the one named last changes fastest.
Arguments:
- picture_embedding_matrix: float32 [32768, 1152], P(('group', 'blk')), parts along dimension 0, may hold values from -0.1875 to 0.1875
- caption_embedding_matrix: float32 [32768, 1152], P(('group', 'blk')), parts along dimension 0, may hold values from -0.1875 to 0.1875
- sharpness_scale: float32 [1], replicated, may hold values from 5 to 15
- offset_shift_vector: float32 [1], replicated, may hold values from -3 to -1
Outputs:
- loss_rows: float32 [32768], P(('group', 'blk')), parts along dimension 0
- grad_image: float32 [32768, 1152], P(('group', 'blk')), parts along dimension 0
- grad_text: float32 [32768, 1152], P(('group', 'blk')), parts along dimension 0
The draws below stay inside these ranges and needn't reach their ends.
There are 8 independent parts, one for each index of `group`. The reference program is written for one: setup_inputs(seed, part) draws one part's arguments, and reference() takes and returns one part's arrays. A program takes and returns all parts, laid end to end along the dimension named above; an argument that names none is the same for every part. Nothing has to cross between parts.
All inputs are finite; a program needn't handle non-finite values.
Results may differ from the reference program's by a relative error of at most 0.014.
Values may be sent and summed in bfloat16 or wider, within the bound.
No kernel may reach another device: no remote copies, remote signals or barrier semaphores. Data moves between devices by JAX's collectives and lax.ppermute only.
A program may use at most 128 MiB of HBM per device.

```python
import math
import jax
import jax.numpy as jnp
from jax import lax

D = 1152
BATCH = 4096


def shard_levels(key, extent, split, smallest, largest):
    factor_of, own = 1.0, jax.random.fold_in(key, 6)
    for axis_at, blocks in split:
        heights = jnp.exp(jax.random.uniform(jax.random.fold_in(own, axis_at), (blocks,), jnp.float32, smallest / len(split), largest / len(split)))
        factor_of = factor_of * jnp.repeat(heights, extent[axis_at] // blocks).reshape([-1 if axis == axis_at else 1 for axis in range(len(extent))])
    return factor_of


def noise(rng, dims, width, bound, cuts=(), held_as=jnp.bfloat16):
    entries = jax.random.normal(rng, dims, jnp.float32) * width
    if len(cuts) > 0:
        entries = shard_levels(rng, dims, cuts, -0.22, 0.18) * entries
    return jnp.clip(entries, min=-bound, max=bound).astype(held_as)


def setup_inputs(seed: int = 0, part: int = 0) -> dict:
    arg_keys = jax.random.split(jax.random.key(seed), 5)
    own_keys = jax.random.split(jax.random.fold_in(arg_keys[4], part), 5)
    return {
        "picture_embedding_matrix": noise(own_keys[0], (BATCH, D), 0.03, 0.1875, ((0, 32),), jnp.float32),
        "caption_embedding_matrix": noise(own_keys[1], (BATCH, D), 0.03, 0.1875, ((0, 32),), jnp.float32),
        "sharpness_scale": jnp.clip(jnp.exp(jax.random.uniform(arg_keys[2], (1,), jnp.float32, math.log(5.0), math.log(15.0))), 5.0, 15.0),
        "offset_shift_vector": jnp.clip(jax.random.uniform(arg_keys[3], (1,), jnp.float32, -3.0, -1.0), -3.0, -1.0),
    }


def normalize(feats):
    scale = 1.0 / jnp.sqrt(lax.optimization_barrier(jnp.sum(feats * feats, axis=1, keepdims=True)) + 1e-06)
    return (feats * scale, scale)

def back_norm(hat, scale, grad):
    return scale * (grad - hat * lax.optimization_barrier(jnp.sum(hat * grad, axis=1, keepdims=True)))

def reference(picture_embedding_matrix, caption_embedding_matrix, sharpness_scale, offset_shift_vector):
    image_hat, image_scale = normalize(picture_embedding_matrix)
    text_hat, text_scale = normalize(caption_embedding_matrix)
    picture_gradient_total = image_hat.astype(jnp.bfloat16)
    caption_gradient_total = text_hat.astype(jnp.bfloat16)
    cosine_scores = lax.dot_general(picture_gradient_total, caption_gradient_total, (((1,), (1,)), ((), ())), preferred_element_type=jnp.float32)
    match_scores = sharpness_scale[0] * cosine_scores + offset_shift_vector[0]
    count = picture_embedding_matrix.shape[0]
    ident = jnp.arange(count, dtype=jnp.int32)
    match_polarity = jnp.where(ident[:, None] == ident[None, :], jnp.float32(1.0), jnp.float32(-1.0))
    loss_rows = -lax.optimization_barrier(jnp.sum(jax.nn.log_sigmoid(match_polarity * match_scores), axis=1))
    match_weight_factor = (-match_polarity * jax.nn.sigmoid(-match_polarity * match_scores) * sharpness_scale[0]).astype(jnp.bfloat16)
    hat_grad_image = jnp.dot(match_weight_factor, caption_gradient_total, preferred_element_type=jnp.float32)
    hat_grad_text = lax.dot_general(match_weight_factor, picture_gradient_total, (((0,), (0,)), ((), ())), preferred_element_type=jnp.float32)
    grad_image = back_norm(image_hat, image_scale, hat_grad_image)
    grad_text = back_norm(text_hat, text_scale, hat_grad_text)
    return (loss_rows, grad_image, grad_text)
```

```python
import jax
import jax.numpy as jnp
from jax import lax
from jax.sharding import PartitionSpec as P

BF16 = jnp.bfloat16
F32 = jnp.float32
RING = 8
PLANE = 4


def along_z(rows, distance):
    route = [
        (z * PLANE + q, ((z + distance) % RING) * PLANE + q)
        for z in range(RING)
        for q in range(PLANE)
    ]
    return lax.ppermute(rows, "blk", route)


def across_x(rows):
    return lax.ppermute(rows, "blk", [(i, i ^ 2) for i in range(RING * PLANE)])


def across_core(rows):
    return lax.ppermute(rows, "blk", [(i, i ^ 1) for i in range(RING * PLANE)])


def normalize(feats):
    scale = 1.0 / jnp.sqrt(jnp.sum(feats * feats, axis=1, keepdims=True) + 1e-06)
    return (feats * scale, scale)


def back_norm(hat, scale, grad):
    return scale * (grad - hat * jnp.sum(hat * grad, axis=1, keepdims=True))


def plane_rows(rows):
    beside = across_x(rows)
    return jnp.concatenate([rows, across_core(rows), beside, across_core(beside)], 0)


def scores(mine, block, sharpness, shift):
    dots = lax.dot_general(
        mine, block, (((1,), (1,)), ((), ())), preferred_element_type=F32
    )
    return sharpness * dots + shift


def away_terms(mine, block, sharpness, shift, with_loss):
    logits = scores(mine, block, sharpness, shift)
    coeff = (jax.nn.sigmoid(logits) * sharpness).astype(BF16)
    grad = jnp.dot(coeff, block, preferred_element_type=F32)
    loss = jnp.sum(jax.nn.softplus(logits), axis=1) if with_loss else None
    return grad, loss


def home_terms(mine, block, sharpness, shift, with_loss):
    logits = scores(mine, block, sharpness, shift)
    n = block.shape[0]
    row = lax.broadcasted_iota(jnp.int32, logits.shape, 0)
    col = lax.broadcasted_iota(jnp.int32, logits.shape, 1)
    sign = jnp.where(row == col, F32(1.0), F32(-1.0))
    coeff = (-sign * jax.nn.sigmoid(-sign * logits) * sharpness).astype(BF16)
    grad = jnp.dot(coeff, block, preferred_element_type=F32)
    loss = jnp.sum(jax.nn.softplus(-sign * logits), axis=1) if with_loss else None
    return grad, loss


def gather_z(rows):
    half = rows.shape[0] // 2
    right = left = rows
    steps = []
    for _ in range(RING // 2 - 1):
        right, left = along_z(right, 1), along_z(left, -1)
        steps.append((right, left))
    steps.append((along_z(right[:half], 1), along_z(left[half:], -1)))
    return steps


def side(mine, own, steps, sharpness, shift, with_loss):
    grad, loss = home_terms(mine, own, sharpness, shift, with_loss)
    for pair in steps:
        more, more_loss = away_terms(
            mine, jnp.concatenate(pair, 0), sharpness, shift, with_loss
        )
        grad = grad + more
        if with_loss:
            loss = loss + more_loss
    return grad, loss


def sum_over_plane(part, n, sent_as):
    part = part.reshape((4, n) + part.shape[1:])
    for_core = part[1::2].astype(sent_as)
    kept = part[0::2] + across_core(for_core).astype(F32)
    return kept[0] + across_x(kept[1].astype(sent_as)).astype(F32)


def body(pictures, captions, sharpness_scale, offset_shift_vector):
    sharpness, shift = sharpness_scale[0], offset_shift_vector[0]
    n = pictures.shape[0]
    text_hat, text_scale = normalize(captions)
    text_low = text_hat.astype(BF16)
    image_hat, image_scale = normalize(pictures)
    image_low = image_hat.astype(BF16)

    text_steps = gather_z(text_low)
    images = plane_rows(image_low)
    image_steps = gather_z(image_low)
    texts = plane_rows(text_low)

    part_image, part_loss = side(images, text_low, text_steps, sharpness, shift, True)
    loss_rows = sum_over_plane(part_loss, n, F32)
    grad_image = back_norm(image_hat, image_scale, sum_over_plane(part_image, n, BF16))

    part_text, _ = side(texts, image_low, image_steps, sharpness, shift, False)
    grad_text = back_norm(text_hat, text_scale, sum_over_plane(part_text, n, BF16))
    return (loss_rows, grad_image, grad_text)


def solution(mesh):
    in_specs = (P(("group", "blk"), None), P(("group", "blk"), None), P(), P())
    out_specs = (P(("group", "blk")), P(("group", "blk"), None), P(("group", "blk"), None))
    return jax.shard_map(body, mesh=mesh, in_specs=in_specs, out_specs=out_specs, check_vma=False)
```

```python
import functools

import jax
import jax.numpy as jnp
from jax import lax
from jax.experimental import pallas as pl
from jax.experimental.pallas import tpu as pltpu
from jax.sharding import PartitionSpec as P

BF16 = jnp.bfloat16
F32 = jnp.float32
RING = 8
PLANE = 4
EXTRA = 16
SMEM = pl.BlockSpec(memory_space=pltpu.SMEM)
VMEM = pl.BlockSpec(memory_space=pltpu.VMEM)


def along_z(rows):
    route = [
        (z * PLANE + q, ((z + (-1 if q % 2 else 1)) % RING) * PLANE + q)
        for z in range(RING)
        for q in range(PLANE)
    ]
    return lax.ppermute(rows, "blk", route)


def across_x(rows):
    return lax.ppermute(rows, "blk", [(i, i ^ 2) for i in range(RING * PLANE)])


def across_core(rows):
    return lax.ppermute(rows, "blk", [(i, i ^ 1) for i in range(RING * PLANE)])


def run(kernel, ins, outs, scalars=(), flops=0, in_place=None):
    shapes = [
        pltpu.VMEM(shape, dtype) if near else jax.ShapeDtypeStruct(shape, dtype)
        for shape, dtype, near in outs
    ]
    ins = [pltpu.with_memory_space_constraint(a, pltpu.VMEM) for a in ins]
    return pl.pallas_call(
        kernel,
        out_shape=shapes,
        in_specs=[SMEM] * len(scalars) + [VMEM] * len(ins),
        out_specs=[VMEM] * len(shapes),
        input_output_aliases=in_place or {},
        cost_estimate=pl.CostEstimate(flops=flops, bytes_accessed=0, transcendentals=0),
        compiler_params=pltpu.CompilerParams(vmem_limit_bytes=24 << 20),
    )(*scalars, *ins)


def hat_of(feats):
    scale = 1.0 / jnp.sqrt(jnp.sum(feats * feats, axis=1, keepdims=True) + 1e-06)
    return feats * scale, scale


def normalize_kernel(*refs):
    for feats_ref, low_ref in zip(refs[:2], refs[2:]):
        low_ref[...] = hat_of(feats_ref[...])[0].astype(BF16)


def normalize(captions, pictures):
    return run(normalize_kernel, [captions, pictures], [(captions.shape, BF16, True)] * 2)


def terms(mine, block, sharpness, shift, with_loss, home):
    dots = lax.dot_general(
        mine, block, (((1,), (1,)), ((), ())), preferred_element_type=F32
    )
    logits = sharpness * dots + shift
    e = jnp.exp(-jnp.abs(logits))
    t = 1.0 / (1.0 + e)
    upper = logits >= 0.0
    coeff = jnp.where(upper, t, e * t) * sharpness
    if home is not None:
        row = lax.broadcasted_iota(jnp.int32, logits.shape, 0) + home
        col = lax.broadcasted_iota(jnp.int32, logits.shape, 1)
        partner = row == col
        coeff = jnp.where(partner, -(jnp.where(upper, e * t, t) * sharpness), coeff)
        logits = jnp.where(partner, -logits, logits)
    loss = jnp.maximum(logits, 0.0) + jnp.log1p(e) if with_loss else None
    return coeff.astype(BF16), loss


def step_kernel(n, blocks, first, last, with_loss, chip_first, scale_ref, shift_ref, *refs):
    refs = list(refs)
    sharpness, shift = scale_ref[0], shift_ref[0]
    block_refs = [refs.pop(0) for _ in range(blocks)]
    if first:
        parts = [refs.pop(0) for _ in range(PLANE)]
        mine_ref = refs.pop(0)
        for k, part in enumerate(parts):
            mine_ref[pl.ds(k * n, n), :] = part[...]
    else:
        mine_ref, before_ref = refs.pop(0), refs.pop(0)
        loss_before_ref = refs.pop(0) if with_loss else None
    total_ref = refs.pop(0)
    loss_ref = refs.pop(0) if with_loss else None
    block = block_refs[0][...]
    if blocks > 1:
        block = jnp.concatenate([b[...] for b in block_refs], 0)
    chunk = 2 * n
    losses = []
    for k in range(PLANE * n // chunk):
        rows = pl.ds(k * chunk, chunk)
        coeff, loss = terms(
            mine_ref[rows, :], block, sharpness, shift, with_loss, k * chunk if first else None
        )
        total = jnp.dot(coeff, block, preferred_element_type=F32)
        if not first:
            total = total + before_ref[rows, :]
        if last and chip_first:
            if k == 0:
                total_ref[...] = total
            else:
                refs[0][pl.ds(0, chunk), :] = total.astype(BF16)
        elif last:
            total_ref[pl.ds(k * n, n), :] = total[:n]
            refs[0][pl.ds(k * n, n), :] = total[n:].astype(BF16)
        else:
            total_ref[rows, :] = total
        if with_loss:
            loss = functools.reduce(
                jnp.add, [loss[:, c * n : c * n + n] for c in range(loss.shape[1] // n)]
            )
            if not first:
                loss = loss + loss_before_ref[rows, :]
            if last:
                losses.append(jnp.sum(loss.T, axis=0, keepdims=True))
            else:
                loss_ref[rows, :] = loss
    if last:
        out_ref = refs[0]
        out_ref[pl.ds(2 * n, EXTRA), :] = jnp.zeros((EXTRA, out_ref.shape[1]), BF16)
        if with_loss:
            mine, theirs = losses
            if not chip_first:
                mine = jnp.concatenate([l[:, :n] for l in losses], 1)
                theirs = jnp.concatenate([l[:, n:] for l in losses], 1)
            loss_ref[...] = jnp.broadcast_to(mine, loss_ref.shape)
            out_ref[pl.ds(2 * n, EXTRA), pl.ds(0, 2 * n)] = in_three(theirs)


def in_three(value):
    high = value.astype(BF16)
    rest = value - high.astype(F32)
    middle = rest.astype(BF16)
    low = (rest - middle.astype(F32)).astype(BF16)
    row = lax.broadcasted_iota(jnp.int32, (EXTRA, value.shape[1]), 0)
    parts = jnp.zeros((EXTRA, value.shape[1]), F32)
    for k, part in enumerate((high, middle, low)):
        parts = jnp.where(row == k, part.astype(F32), parts)
    return parts.astype(BF16)


def from_three(rows):
    return jnp.sum(rows.astype(F32), axis=0, keepdims=True)


def step(blocks, mine, scalars, n, total=None, loss=None, with_loss=False, last=False, chip_first=False):
    width = blocks[0].shape[1]
    first = total is None
    ins = list(blocks) + (list(mine) if first else [mine, total])
    if with_loss and not first:
        ins.append(loss)
    outs = [((PLANE * n, width), BF16, True)] if first else []
    if last:
        outs += [((2 * n, width), F32, True)]
        outs += [((8, 2 * n), F32, True)] if with_loss else []
        outs += [((2 * n + EXTRA, width), BF16, True)]
    else:
        outs += [((PLANE * n, width), F32, True)]
        outs += [((PLANE * n, n), F32, True)] if with_loss else []
    flops = 0
    kernel = functools.partial(step_kernel, n, len(blocks), first, last, with_loss, chip_first)
    return run(kernel, ins, outs, scalars, flops)


def pass_on_kernel(n, with_loss, kept_ref, *refs):
    loss_ref = refs[0] if with_loss else None
    got_ref, out_ref = refs[int(with_loss) : int(with_loss) + 2]
    other = kept_ref[pl.ds(n, n), :] + got_ref[pl.ds(n, n), :].astype(F32)
    out_ref[...] = other.astype(BF16)
    if with_loss:
        loss = loss_ref[0:1, pl.ds(n, n)] + from_three(got_ref[pl.ds(2 * n, EXTRA), pl.ds(n, n)])
        refs[-1][...] = in_three(loss)


def finish_kernel(n, with_loss, feats_ref, kept_ref, *refs):
    first_ref, second_ref = refs[:2]
    grad_ref = refs[4] if with_loss else refs[2]
    grad = (
        kept_ref[pl.ds(0, n), :]
        + first_ref[pl.ds(0, n), :].astype(F32)
        + second_ref[...].astype(F32)
    )
    hat, scale = hat_of(feats_ref[...])
    grad_ref[...] = scale * (grad - hat * jnp.sum(hat * grad, axis=1, keepdims=True))
    if with_loss:
        loss_ref, third_ref = refs[2:4]
        refs[5][...] = (
            loss_ref[0:1, pl.ds(0, n)]
            + from_three(first_ref[pl.ds(2 * n, EXTRA), pl.ds(0, n)])
            + from_three(third_ref[...])
        )


def pass_on(kept, got, loss=None):
    n, width = kept.shape[0] // 2, kept.shape[1]
    with_loss = loss is not None
    outs = [((n, width), BF16, True)] + ([((EXTRA, n), BF16, True)] if with_loss else [])
    return run(
        functools.partial(pass_on_kernel, n, with_loss),
        [kept, *([loss] if with_loss else []), got],
        outs,
    )


def finish(feats, kept, first, second, *losses):
    n, width = feats.shape
    with_loss = len(losses) > 0
    outs = [((n, width), F32, False)] + ([((1, n), F32, False)] if with_loss else [])
    return run(
        functools.partial(finish_kernel, n, with_loss),
        [feats, kept, first, second, *losses],
        outs,
    )


def after(value, *done):
    return lax.optimization_barrier((value, *done))[0]


def body(pictures, captions, sharpness_scale, offset_shift_vector):
    n = pictures.shape[0]
    scalars = (sharpness_scale, offset_shift_vector)
    text, image = normalize(captions, pictures)
    text_core, image_core = across_core(text), across_core(image)
    ta1, tb1 = along_z(text), along_z(text_core)
    ia1 = along_z(image)
    image_chip = across_x(image)
    images = [image, image_core, image_chip, across_core(image_chip)]
    text_chip = across_x(after(text, image_chip))
    texts = [text, text_core, text_chip, across_core(text_chip)]
    ta2 = along_z(ta1)
    tb2 = along_z(tb1)
    ib1 = along_z(after(image_core, ia1))
    mine_i, a0, loss = step([after(text, ia1)], images, scalars, n, with_loss=True)
    ta3 = along_z(ta2)
    a1, loss = step([ta1, after(tb1, ta2)], mine_i, scalars, n, a0, loss, True)
    tb3 = along_z(after(tb2, a0))
    a2, loss = step([ta2, after(tb2, text_chip)], mine_i, scalars, n, a1, loss, True)
    ta4 = along_z(after(ta3, a0))
    ia2 = along_z(after(ia1, ib1))
    mine_t, b0 = step([after(image, ib1)], texts, scalars, n)
    b1, = step([ia1, ib1], mine_t, scalars, n, b0)
    ib2 = along_z(after(ib1, ta3))
    ia3 = along_z(ia2)
    a3, loss = step([ta3, tb3], mine_i, scalars, n, a2, loss, True)
    ib3 = along_z(ib2)
    kept_i, loss, for_chip_i = step([ta4], mine_i, scalars, n, a3, loss, True, True, True)
    by_chip_i = across_x(for_chip_i)
    ia4 = along_z(ia3)
    b2, = step([ia2, ib2], mine_t, scalars, n, b1)
    b3, = step([ia3, ib3], mine_t, scalars, n, b2)
    kept, for_core = step([after(ia4, by_chip_i)], mine_t, scalars, n, b3, last=True)
    by_core = across_core(for_core)
    for_chip = pass_on(kept, by_core)[0]
    by_chip = across_x(for_chip)
    for_core_i, loss_low = pass_on(after(kept_i, for_chip), by_chip_i, loss)
    by_core_i = across_core(for_core_i)
    loss_by_core = across_core(loss_low)
    grad_image, loss_rows = finish(pictures, kept_i, by_chip_i, by_core_i, loss, loss_by_core)

    grad_text = finish(after(captions, grad_image), kept, by_core, by_chip)[0]
    return (loss_rows.reshape(n), grad_image, grad_text)


def solution(mesh):
    in_specs = (P(("group", "blk"), None), P(("group", "blk"), None), P(), P())
    out_specs = (P(("group", "blk")), P(("group", "blk"), None), P(("group", "blk"), None))
    return jax.shard_map(body, mesh=mesh, in_specs=in_specs, out_specs=out_specs, check_vma=False)
```

```python
import functools

import jax
import jax.numpy as jnp
from jax import lax
from jax.experimental import pallas as pl
from jax.experimental.pallas import tpu as pltpu
from jax.sharding import PartitionSpec as P

BF16 = jnp.bfloat16
F32 = jnp.float32
RING = 8
PLANE = 4
EXTRA = 16
SMEM = pl.BlockSpec(memory_space=pltpu.SMEM)
VMEM = pl.BlockSpec(memory_space=pltpu.VMEM)


def along_z(rows):
    route = [
        (z * PLANE + q, ((z + (-1 if q % 2 else 1)) % RING) * PLANE + q)
        for z in range(RING)
        for q in range(PLANE)
    ]
    return lax.ppermute(rows, "blk", route)


def across_x(rows):
    return lax.ppermute(rows, "blk", [(i, i ^ 2) for i in range(RING * PLANE)])


def across_core(rows):
    return lax.ppermute(rows, "blk", [(i, i ^ 1) for i in range(RING * PLANE)])


def run(kernel, ins, outs, scalars=(), flops=0, in_place=None):
    shapes = [
        pltpu.VMEM(shape, dtype) if near else jax.ShapeDtypeStruct(shape, dtype)
        for shape, dtype, near in outs
    ]
    ins = [pltpu.with_memory_space_constraint(a, pltpu.VMEM) for a in ins]
    return pl.pallas_call(
        kernel,
        out_shape=shapes,
        in_specs=[SMEM] * len(scalars) + [VMEM] * len(ins),
        out_specs=[VMEM] * len(shapes),
        input_output_aliases=in_place or {},
        cost_estimate=pl.CostEstimate(flops=flops, bytes_accessed=0, transcendentals=0),
        compiler_params=pltpu.CompilerParams(vmem_limit_bytes=24 << 20),
    )(*scalars, *ins)


def hat_of(feats):
    scale = 1.0 / jnp.sqrt(jnp.sum(feats * feats, axis=1, keepdims=True) + 1e-06)
    return feats * scale, scale


def normalize_kernel(*refs):
    for feats_ref, low_ref in zip(refs[:2], refs[2:]):
        low_ref[...] = hat_of(feats_ref[...])[0].astype(BF16)


def normalize(captions, pictures):
    return run(normalize_kernel, [captions, pictures], [(captions.shape, BF16, True)] * 2)


def terms(mine, block, sharpness, shift, with_loss, home):
    dots = lax.dot_general(
        mine, block, (((1,), (1,)), ((), ())), preferred_element_type=F32
    )
    logits = sharpness * dots + shift
    e = jnp.exp(-jnp.abs(logits))
    t = 1.0 / (1.0 + e)
    upper = logits >= 0.0
    coeff = jnp.where(upper, t, e * t) * sharpness
    if home is not None:
        row = lax.broadcasted_iota(jnp.int32, logits.shape, 0) + home
        col = lax.broadcasted_iota(jnp.int32, logits.shape, 1)
        partner = row == col
        coeff = jnp.where(partner, -(jnp.where(upper, e * t, t) * sharpness), coeff)
        logits = jnp.where(partner, -logits, logits)
    loss = jnp.maximum(logits, 0.0) + jnp.log1p(e) if with_loss else None
    return coeff.astype(BF16), loss


def step_kernel(n, blocks, first, last, with_loss, chip_first, scale_ref, shift_ref, *refs):
    refs = list(refs)
    sharpness, shift = scale_ref[0], shift_ref[0]
    block_refs = [refs.pop(0) for _ in range(blocks)]
    if first:
        parts = [refs.pop(0) for _ in range(PLANE)]
        mine_ref = refs.pop(0)
        for k, part in enumerate(parts):
            mine_ref[pl.ds(k * n, n), :] = part[...]
    else:
        mine_ref, before_ref = refs.pop(0), refs.pop(0)
        loss_before_ref = refs.pop(0) if with_loss else None
    total_ref = refs.pop(0)
    loss_ref = refs.pop(0) if with_loss else None
    block = block_refs[0][...]
    if blocks > 1:
        block = jnp.concatenate([b[...] for b in block_refs], 0)
    chunk = 2 * n
    losses = []
    for k in range(PLANE * n // chunk):
        rows = pl.ds(k * chunk, chunk)
        coeff, loss = terms(
            mine_ref[rows, :], block, sharpness, shift, with_loss, k * chunk if first else None
        )
        total = jnp.dot(coeff, block, preferred_element_type=F32)
        if not first:
            total = total + before_ref[rows, :]
        if last and chip_first:
            if k == 0:
                total_ref[...] = total
            else:
                refs[0][pl.ds(0, chunk), :] = total.astype(BF16)
        elif last:
            total_ref[pl.ds(k * n, n), :] = total[:n]
            refs[0][pl.ds(k * n, n), :] = total[n:].astype(BF16)
        else:
            total_ref[rows, :] = total
        if with_loss:
            loss = functools.reduce(
                jnp.add, [loss[:, c * n : c * n + n] for c in range(loss.shape[1] // n)]
            )
            if not first:
                loss = loss + loss_before_ref[rows, :]
            if last:
                losses.append(jnp.sum(loss.T, axis=0, keepdims=True))
            else:
                loss_ref[rows, :] = loss
    if last:
        out_ref = refs[0]
        out_ref[pl.ds(2 * n, EXTRA), :] = jnp.zeros((EXTRA, out_ref.shape[1]), BF16)
        if with_loss:
            mine, theirs = losses
            if not chip_first:
                mine = jnp.concatenate([l[:, :n] for l in losses], 1)
                theirs = jnp.concatenate([l[:, n:] for l in losses], 1)
            loss_ref[...] = jnp.broadcast_to(mine, loss_ref.shape)
            out_ref[pl.ds(2 * n, EXTRA), pl.ds(0, 2 * n)] = in_three(theirs)


def in_three(value):
    high = value.astype(BF16)
    rest = value - high.astype(F32)
    middle = rest.astype(BF16)
    low = (rest - middle.astype(F32)).astype(BF16)
    row = lax.broadcasted_iota(jnp.int32, (EXTRA, value.shape[1]), 0)
    parts = jnp.zeros((EXTRA, value.shape[1]), F32)
    for k, part in enumerate((high, middle, low)):
        parts = jnp.where(row == k, part.astype(F32), parts)
    return parts.astype(BF16)


def from_three(rows):
    return jnp.sum(rows.astype(F32), axis=0, keepdims=True)


def step(blocks, mine, scalars, n, total=None, loss=None, with_loss=False, last=False, chip_first=False):
    width = blocks[0].shape[1]
    first = total is None
    ins = list(blocks) + (list(mine) if first else [mine, total])
    if with_loss and not first:
        ins.append(loss)
    outs = [((PLANE * n, width), BF16, True)] if first else []
    if last:
        outs += [((2 * n, width), F32, True)]
        outs += [((8, 2 * n), F32, True)] if with_loss else []
        outs += [((2 * n + EXTRA, width), BF16, True)]
    else:
        outs += [((PLANE * n, width), F32, True)]
        outs += [((PLANE * n, n), F32, True)] if with_loss else []
    flops = 0
    kernel = functools.partial(step_kernel, n, len(blocks), first, last, with_loss, chip_first)
    return run(kernel, ins, outs, scalars, flops)


def pass_on_kernel(n, with_loss, kept_ref, *refs):
    loss_ref = refs[0] if with_loss else None
    got_ref, out_ref = refs[int(with_loss) : int(with_loss) + 2]
    other = kept_ref[pl.ds(n, n), :] + got_ref[pl.ds(n, n), :].astype(F32)
    out_ref[...] = other.astype(BF16)
    if with_loss:
        loss = loss_ref[0:1, pl.ds(n, n)] + from_three(got_ref[pl.ds(2 * n, EXTRA), pl.ds(n, n)])
        refs[-1][...] = in_three(loss)


def finish_kernel(n, with_loss, feats_ref, kept_ref, *refs):
    first_ref, second_ref = refs[:2]
    grad_ref = refs[4] if with_loss else refs[2]
    grad = (
        kept_ref[pl.ds(0, n), :]
        + first_ref[pl.ds(0, n), :].astype(F32)
        + second_ref[...].astype(F32)
    )
    hat, scale = hat_of(feats_ref[...])
    grad_ref[...] = scale * (grad - hat * jnp.sum(hat * grad, axis=1, keepdims=True))
    if with_loss:
        loss_ref, third_ref = refs[2:4]
        refs[5][...] = (
            loss_ref[0:1, pl.ds(0, n)]
            + from_three(first_ref[pl.ds(2 * n, EXTRA), pl.ds(0, n)])
            + from_three(third_ref[...])
        )


def pass_on(kept, got, loss=None):
    n, width = kept.shape[0] // 2, kept.shape[1]
    with_loss = loss is not None
    outs = [((n, width), BF16, True)] + ([((EXTRA, n), BF16, True)] if with_loss else [])
    return run(
        functools.partial(pass_on_kernel, n, with_loss),
        [kept, *([loss] if with_loss else []), got],
        outs,
    )


def finish(feats, kept, first, second, *losses):
    n, width = feats.shape
    with_loss = len(losses) > 0
    outs = [((n, width), F32, False)] + ([((1, n), F32, False)] if with_loss else [])
    return run(
        functools.partial(finish_kernel, n, with_loss),
        [feats, kept, first, second, *losses],
        outs,
    )


def after(value, *done):
    return lax.optimization_barrier((value, *done))[0]


def body(pictures, captions, sharpness_scale, offset_shift_vector):
    n = pictures.shape[0]
    scalars = (sharpness_scale, offset_shift_vector)
    text, image = normalize(captions, pictures)
    text_core, image_core = across_core(text), across_core(image)
    ta1, tb1 = along_z(text), along_z(text_core)
    ia1 = along_z(image)
    image_chip = across_x(image)
    images = [image, image_core, image_chip, across_core(image_chip)]
    text_chip = across_x(after(text, image_chip))
    texts = [text, text_core, text_chip, across_core(text_chip)]
    ta2 = along_z(ta1)
    tb2 = along_z(tb1)
    ib1 = along_z(after(image_core, ia1))
    mine_i, a0, loss = step([after(text, ia1)], images, scalars, n, with_loss=True)
    ta3 = along_z(ta2)
    a1, loss = step([ta1, after(tb1, ta2)], mine_i, scalars, n, a0, loss, True)
    tb3 = along_z(after(tb2, a0))
    a2, loss = step([ta2, after(tb2, text_chip)], mine_i, scalars, n, a1, loss, True)
    ta4 = along_z(after(ta3, a0))
    ia2 = along_z(after(ia1, tb1))
    mine_t, b0 = step([after(image, ib1)], texts, scalars, n)
    b1, = step([ia1, ib1], mine_t, scalars, n, b0)
    ib2 = along_z(after(ib1, tb2))
    ia3 = along_z(ia2)
    a3, loss = step([ta3, tb3], mine_i, scalars, n, a2, loss, True)
    ib3 = along_z(after(ib2, b1))
    kept_i, loss, for_chip_i = step([ta4], mine_i, scalars, n, a3, loss, True, True, True)
    by_chip_i = across_x(for_chip_i)
    ia4 = along_z(ia3)
    b2, = step([ia2, ib2], mine_t, scalars, n, b1)
    b3, = step([ia3, ib3], mine_t, scalars, n, b2)
    kept, for_core = step([after(ia4, by_chip_i)], mine_t, scalars, n, b3, last=True)
    by_core = across_core(for_core)
    for_chip = pass_on(kept, by_core)[0]
    by_chip = across_x(for_chip)
    for_core_i, loss_low = pass_on(after(kept_i, for_chip), by_chip_i, loss)
    by_core_i = across_core(for_core_i)
    loss_by_core = across_core(loss_low)
    grad_image, loss_rows = finish(pictures, kept_i, by_chip_i, by_core_i, loss, loss_by_core)

    grad_text = finish(after(captions, grad_image), kept, by_core, by_chip)[0]
    return (loss_rows.reshape(n), grad_image, grad_text)


def solution(mesh):
    in_specs = (P(("group", "blk"), None), P(("group", "blk"), None), P(), P())
    out_specs = (P(("group", "blk")), P(("group", "blk"), None), P(("group", "blk"), None))
    return jax.shard_map(body, mesh=mesh, in_specs=in_specs, out_specs=out_specs, check_vma=False)
```
